512 devices in a mesh: sec: 8 (over y, core), fsdp: 64 (over z, x).
Axes of the slice: x: 4, y: 4, z: 16, core: 2. Of those that a mesh axis runs over, the one named last changes fastest.
Arguments:
- tokens: bfloat16 [16384, 2048], P('fsdp', 'sec'), may hold values from -6 to 6
- routes: int32 [16384, 2], P('fsdp'), may hold values from 0 to 63, all different within a row; in each aligned block of 128 rows (0 to 127, 128 to 255, ...) at most 8 rows name the same one
- gate_weights: float32 [16384, 2], P('fsdp'), may hold values from 0.1 to 1
- pad_mask: int32 [16384], P('fsdp'), may hold values 0 or 1
- expand_weight: bfloat16 [64, 2048, 4096], P('fsdp', None, 'sec'), may hold values from -0.125 to 0.125
- shrink_weight: bfloat16 [64, 4096, 2048], P('fsdp', 'sec'), may hold values from -0.125 to 0.125
Outputs:
- mixed: bfloat16 [16384, 2048], P('fsdp', 'sec')
The draws below stay inside these ranges and needn't reach their ends.
Inputs may be any that keep to these rules, and one draw needn't show every extreme that they name: `routes`: in each aligned block of 128 rows no expert is named by more than 8 rows, and the two experts of a row differ.
All inputs are finite; a program needn't handle non-finite values. No bound on the sum of `pad_mask` on one device may be relied on, other than what follows from the above.
Results may differ from the reference program's by a relative error of at most 0.019.
Values may be sent and summed in bfloat16 or wider, within the bound.
A program may use at most 64 MiB of HBM per device.

```python
import math
import jax
import jax.numpy as jnp
import numpy as np
from jax import lax

D = 2048
FF = 4096
TOK_DEV = 256
BLOCK = 128
EXPERTS = 64
MOST = 8
CAP = 16
FF_DEV = 512
TOKENS = 16384
N_SEC = 8
N_FSDP = 64


def touch_ends(drawn, own_key, smallest, largest):
    longest = drawn.shape.index(max(drawn.shape))
    spots = []
    for shift in (0, 1):
        where = [jax.random.randint(jax.random.fold_in(own_key, axis), (), 0, length) for axis, length in enumerate(drawn.shape)]
        where[longest] = (where[longest] + shift) % drawn.shape[longest]
        spots.append(tuple(where))
    return drawn.at[spots[0]].set(smallest).at[spots[1]].set(largest)


def strengthened(values, key, source, target, parts, factor):
    owner, partner = [(jnp.arange(values.shape[position]) // (values.shape[position] // parts)).reshape([-1 if axis == position else 1 for axis in range(values.ndim)]) for position in (source, target)]
    chosen = jax.random.permutation(key, parts)[partner]
    strong = (owner == chosen) | (owner == (partner + parts // 2) % parts)
    return jnp.where(strong, factor * values, values)


def steps_of(own_key, extent, pieces, least, largest):
    def one(dim, parts):
        heights = jax.random.uniform(jax.random.fold_in(jax.random.fold_in(own_key, 6), dim), (parts,), jnp.float32, least / len(pieces), largest / len(pieces))
        return jnp.repeat(jnp.exp(heights), extent[dim] // parts).reshape((-1,) + (1,) * (len(extent) - dim - 1))

    level = one(*pieces[0])
    for cut in pieces[1:]:
        level = level * one(*cut)
    return level


def routed_block(rng, own, number, rows, count, top, limit, lean):
    ranking = jax.random.permutation(rng, count)
    heavy_load, common = shares(count, rows * top, limit, lean, True), shares(count, rows * top, limit, lean, False)
    places = jnp.arange(count)

    def named(sizes, offset_by):
        used = int((sizes > 0).sum())
        fixed = max(1, used // 4)
        passed = fixed + (places - fixed + offset_by * (used - fixed)) % max(1, count - fixed)
        return jnp.zeros((count,), jnp.int32).at[ranking[jnp.where(places < fixed, places, passed)]].set(jnp.asarray(sizes, jnp.int32))

    sizes = jnp.where(number % 4 == 0, named(heavy_load, number // 4), named(common, number - number // 4 - 1))
    mixed = jax.random.permutation(jax.random.fold_in(own, 3), count)
    giver, receiver = mixed[0:count // 2 * 2:2], mixed[1:count // 2 * 2:2]
    margin = jnp.minimum(sizes[giver] - 1, limit - sizes[receiver]) // 2
    margin = jnp.where((giver == ranking[0]) | (receiver == ranking[0]) | (sizes[receiver] == 0), 0, jnp.maximum(margin, 0))
    passed = jax.random.randint(jax.random.fold_in(own, 4), (count // 2,), 0, 1 << 20) % (margin + 1)
    sizes = sizes.at[giver].add(-passed).at[receiver].add(passed)
    members = jnp.searchsorted(jnp.cumsum(sizes), jnp.arange(rows * top), side="right").astype(jnp.int32)
    table = members.reshape(top, rows).T
    table = table[jax.random.permutation(jax.random.fold_in(own, 1), rows)]
    offset_by = jax.random.randint(jax.random.fold_in(own, 2), (rows, 1), 0, top)
    return jnp.take_along_axis(table, (jnp.arange(top)[None, :] + offset_by) % top, axis=1)


def shares(count, total, reach, skew, full):
    weights = [(1 << 20) // math.isqrt(grade ** skew) + 1 for grade in range(1, count + 1)]
    largest = reach if full else min(reach, max(-(-total // count), total * weights[0] // sum(weights)))
    least = 1 if total - largest >= count - 1 else 0
    counts, surplus = [largest] + [least] * (count - 1), total - largest - least * (count - 1)
    while surplus > 0:
        movable = [i for i in range(1, count) if counts[i] < largest] or [i for i in range(1, count) if counts[i] < reach]
        mass, left = sum([weights[i] for i in movable]), surplus
        for i in movable:
            extra = min(reach - counts[i], max(1, left * weights[i] // mass), surplus)
            counts[i] = counts[i] + extra
            surplus = surplus - extra
    return np.array(counts)


def centred(own_key, shape, spread, most, cuts=(), kind=jnp.bfloat16):
    factor_of = steps_of(own_key, shape, cuts, -0.22, 0.18) if cuts else 1.0
    array = jax.random.normal(own_key, shape, jnp.float32) * spread * factor_of
    return jnp.minimum(jnp.maximum(array, -most), most).astype(kind)


def heavy_noise(rng, extent, deviation, most, shards, heavy, held_as=jnp.bfloat16):
    values = deviation * jax.random.normal(rng, extent, jnp.float32)
    if shards:
        values = values * steps_of(rng, extent, shards, -0.22, 0.18)
    return jnp.clip(strengthened(values, jax.random.fold_in(rng, 3), *heavy), -most, most).astype(held_as)


def setup_inputs(seed: int = 0) -> dict:
    key_of = jax.random.split(jax.random.key(seed), 7)
    tokens = centred(key_of[0], (TOKENS, D), 1.0, 6.0, ((0, 64), (1, 8)))
    routes_keys = jax.random.split(jax.random.fold_in(key_of[1], 1), TOKENS // BLOCK)
    routes_turns = jax.random.permutation(jax.random.fold_in(key_of[1], 3), TOKENS // BLOCK)
    routes = jax.vmap(lambda own, number: routed_block(jax.random.fold_in(key_of[1], 2), own, number, BLOCK, EXPERTS, 2, MOST, 2))(routes_keys, routes_turns).reshape((TOKENS, 2))
    gate_weights = jnp.clip(0.1 + 0.9 * jax.random.uniform(key_of[2], (TOKENS, 2), jnp.float32) ** steps_of(key_of[2], (TOKENS, 2), ((0, 64),), -0.2, 0.2), 0.1, 1.0)
    pad_mask = touch_ends((jax.random.randint(key_of[3], (TOKENS,), 0, 8) < 7).astype(jnp.int32), jax.random.fold_in(key_of[3], 1), 0, 1)
    expand_weight = centred(key_of[4], (EXPERTS, D, FF), D ** -0.5, 0.125, ((0, 64), (2, 8)))
    shrink_weight = heavy_noise(key_of[5], (EXPERTS, FF, D), FF ** -0.5, 0.125, ((0, 64), (1, 8)), (1, 2, 8, 2.0))
    return dict(tokens=tokens, routes=routes, gate_weights=gate_weights, pad_mask=pad_mask, expand_weight=expand_weight, shrink_weight=shrink_weight)


def slot_targets(route_rows, experts, most, block):
    flat_ids = route_rows.reshape(-1)
    count = flat_ids.shape[0]
    top_k = route_rows.shape[1]
    onehot = (flat_ids[:, None] == jnp.arange(experts, dtype=jnp.int32)[None, :]).astype(jnp.int32)
    blocks = count // (top_k * block)
    running = jnp.cumsum(onehot.reshape(blocks, top_k * block, experts), axis=1).reshape(count, experts)
    rank_in = jnp.sum(onehot * running, axis=1) - 1
    block_ids = jnp.arange(count, dtype=jnp.int32) // (top_k * block)
    capacity = blocks * most
    return (flat_ids * capacity + block_ids * most + rank_in).astype(jnp.int32)


def expert_apply(operands):
    rows, w_a, w_b = operands
    hidden = jnp.maximum(jnp.dot(rows, w_a, preferred_element_type=jnp.float32), 0.0).astype(jnp.bfloat16)
    hidden_blocks = hidden.astype(jnp.float32).reshape(rows.shape[0], N_SEC, FF_DEV)
    weight_blocks = w_b.astype(jnp.float32).reshape(N_SEC, FF_DEV, D)
    partials = jnp.einsum("rjf,jfd->jrd", hidden_blocks, weight_blocks).astype(jnp.bfloat16)
    partials = lax.optimization_barrier(partials)
    return jnp.sum(partials.astype(jnp.float32), axis=0).astype(jnp.bfloat16)


def reference(tokens, routes, gate_weights, pad_mask, expand_weight, shrink_weight):
    grouped = routes.reshape(N_FSDP, TOK_DEV, 2)
    targets = jax.vmap(lambda group: slot_targets(group, EXPERTS, MOST, BLOCK))(grouped)
    expert_ids = targets // CAP
    positions = jnp.arange(N_FSDP, dtype=jnp.int32)[:, None] * CAP + targets % CAP
    repeated = jnp.repeat(tokens, 2, axis=0).reshape(N_FSDP, TOK_DEV * 2, D)
    buffer = jnp.zeros((EXPERTS, N_FSDP * CAP, D), jnp.bfloat16)
    buffer = buffer.at[expert_ids, positions].set(repeated)
    expert_out = lax.map(expert_apply, (buffer, expand_weight, shrink_weight))
    picked = expert_out[expert_ids, positions].astype(jnp.float32).reshape(TOKENS, 2, D)
    scale = gate_weights * pad_mask.astype(jnp.float32)[:, None]
    return jnp.sum(picked * scale[:, :, None], axis=1).astype(jnp.bfloat16)
```

```python
import jax
import jax.numpy as jnp
from jax import lax
from jax.experimental import pallas as pl
from jax.experimental.pallas import tpu as pltpu
from jax.sharding import PartitionSpec as P

MESH = pl.DeviceIdType.MESH
NZ, NX, NY = 16, 4, 4
SLOTS = 16
SHARE = 256
ROWS = NZ * NX * SLOTS
ORDER = (0, 1, 15, 2, 8, 9, 7, 10, 6, 11, 5, 12, 4, 13, 3, 14)
PER = 2
NB = NZ // PER
B = PER * NX * SLOTS
BF = jnp.bfloat16
F32 = jnp.float32


def wait_for(ref, sem):
    pltpu.make_async_copy(ref, ref, sem).wait()


def kernel(tok_hbm, routes_hbm, gates_hbm, mask_hbm, w1_hbm, w2_hbm, out, tok, routes, gates, mask, w1, w2, filled, g, part, sibp, cs, yrecv,
           eo, ret, qhi, qlo, w_sem, d_send, d_recv, a_send, a_recv, s_send, s_recv, p_send, p_recv,
           y_send, y_recv, r_send, r_recv):
    sec = lax.axis_index("sec")
    fs = lax.axis_index("fsdp")
    y, c = sec // 2, sec % 2
    z, x = fs // NX, fs % NX
    sib = (y * 2 + (1 - c), fs)

    def at(dz, dx):
        return (sec, (z + dz) % NZ * NX + (x + dx) % NX)

    def at_y(dy):
        return ((y + dy) % NY * 2 + c, fs)

    pairs = ((routes_hbm, routes), (tok_hbm, tok), (gates_hbm, gates), (mask_hbm, mask))
    loads = [pltpu.make_async_copy(src, dst, w_sem.at[2 + i]) for i, (src, dst) in enumerate(pairs)]
    for load in loads:
        load.start()

    barrier = pltpu.get_barrier_semaphore()
    partners = [at(ORDER[p], dx) for p in reversed(range(NZ)) for dx in range(NX) if (ORDER[p], dx) != (0, 0)]
    partners += [at_y(1), at_y(2), at_y(3), sib]
    for partner in partners:
        pl.semaphore_signal(barrier, inc=1, device_id=partner, device_id_type=MESH)

    load1 = pltpu.make_async_copy(w1_hbm.at[0], w1, w_sem.at[0])
    load2 = pltpu.make_async_copy(w2_hbm.at[0], w2, w_sem.at[1])
    load1.start()
    load2.start()
    for load in loads[:2]:
        load.wait()

    ids = routes[...]
    expert = lax.broadcasted_iota(jnp.int32, (NZ * NX, 256), 0)
    named = [(expert == ids[k:k + 1, :]).astype(F32) for k in range(2)]
    row = lax.broadcasted_iota(jnp.int32, (256, 256), 0)
    col = lax.broadcasted_iota(jnp.int32, (256, 256), 1)
    earlier = ((row < col) & (row // 128 == col // 128)).astype(BF)
    before = jnp.dot((named[0] + named[1]).astype(BF), earlier, preferred_element_type=F32)
    away = (z - (ids >> 2)) & (NZ - 1)
    place = jnp.zeros_like(ids)
    for p, r in enumerate(ORDER):
        place = jnp.where(away == r, p, place)
    half = lax.broadcasted_iota(jnp.int32, (1, 256), 1) // 128
    target = []
    for k in range(2):
        rank = jnp.sum(named[k] * before, axis=0, keepdims=True).astype(jnp.int32)
        target.append(place[k:k + 1, :] * (NX * SLOTS) + (ids[k:k + 1, :] & (NX - 1)) * SLOTS + half * 8 + rank)
    slot = lax.broadcasted_iota(jnp.int32, (ROWS, 256), 0)
    pick = ((slot == target[0]) | (slot == target[1])).astype(BF)
    filled[...] = jnp.dot(pick, tok[...], preferred_element_type=F32).astype(BF).reshape(NZ * NX, SLOTS, SHARE)

    pl.semaphore_wait(barrier, len(partners))

    def rows(b):
        return pl.ds(b * B, B)

    for p, r in enumerate(ORDER):
        for dx in range(NX):
            there = (x + dx) % NX
            src = filled.at[p * NX + there]
            dst = g.at[c, y, pl.ds(pl.multiple_of((p * NX + x) * SLOTS, SLOTS), SLOTS)]
            if (r, dx) == (0, 0):
                pltpu.make_async_copy(src, dst, d_recv.at[p // PER]).start()
            else:
                pltpu.make_async_remote_copy(
                    src_ref=src, dst_ref=dst, send_sem=d_send, recv_sem=d_recv.at[p // PER],
                    device_id=at(NZ - r, dx), device_id_type=MESH).start()

    for load in loads[2:]:
        load.wait()
    scale = gates[...] * mask[...].astype(F32)
    lanes = jnp.concatenate([target[0].astype(F32), target[1].astype(F32), scale, jnp.zeros((124, 256), F32)], axis=0)
    sides = lanes.T
    column = lax.broadcasted_iota(jnp.int32, (256, ROWS), 1)
    q = jnp.where(column == sides[:, 0:1].astype(jnp.int32), sides[:, 2:3], 0.0)
    q = q + jnp.where(column == sides[:, 1:2].astype(jnp.int32), sides[:, 3:4], 0.0)
    high = q.astype(BF)
    qhi[...] = high
    qlo[...] = (q - high.astype(F32)).astype(BF)

    def gather(b):
        wait_for(g.at[c, y, rows(b)], d_recv.at[b])
        own = g.at[c, y, rows(b)]
        for dy in (2, 1, 3):
            pltpu.make_async_remote_copy(
                src_ref=own, dst_ref=own, send_sem=a_send, recv_sem=a_recv.at[b, dy - 1],
                device_id=at_y(dy), device_id_type=MESH).start()
        pltpu.make_async_remote_copy(
            src_ref=own, dst_ref=own, send_sem=s_send, recv_sem=s_recv.at[b],
            device_id=sib, device_id_type=MESH).start()

    def share(b):
        for dy in (1, 3, 2):
            block = g.at[c, (y + NY - dy) % NY, rows(b)]
            wait_for(block, a_recv.at[b, dy - 1])
            pltpu.make_async_remote_copy(
                src_ref=block, dst_ref=block, send_sem=s_send, recv_sem=s_recv.at[b],
                device_id=sib, device_id_type=MESH).start()

    def feed(b):
        wait_for(g.at[1 - c, :, rows(b)], s_recv.at[b])
        if b == 0:
            load1.wait()
            load2.wait()
        xs = jnp.concatenate([g[s % 2, s // 2, rows(b), :] for s in range(8)], axis=1)
        hidden = jnp.maximum(jnp.dot(xs, w1[...], preferred_element_type=F32), 0.0).astype(BF)
        outs = jnp.dot(hidden, w2[...], preferred_element_type=F32).astype(BF)
        for s in range(8):
            part[b, s % 2, s // 2] = outs[:, s * SHARE:(s + 1) * SHARE]
        pltpu.make_async_remote_copy(
            src_ref=part.at[b, 1 - c], dst_ref=sibp.at[b], send_sem=p_send, recv_sem=p_recv.at[b],
            device_id=sib, device_id_type=MESH).start()

    def scatter(b):
        wait_for(sibp.at[b], p_recv.at[b])
        for dy in (2, 1, 3):
            there = (y + dy) % NY
            cs[b, dy - 1] = (part[b, c, there].astype(F32) + sibp[b, there].astype(F32)).astype(BF)
            pltpu.make_async_remote_copy(
                src_ref=cs.at[b, dy - 1], dst_ref=yrecv.at[b, dy - 1], send_sem=y_send,
                recv_sem=y_recv.at[b, dy - 1], device_id=at_y(dy), device_id_type=MESH).start()

    def give_back(b):
        total = part[b, c, y].astype(F32) + sibp[b, y].astype(F32)
        for dy in (1, 3, 2):
            wait_for(yrecv.at[b, dy - 1], y_recv.at[b, dy - 1])
            total = total + yrecv[b, dy - 1].astype(F32)
        eo[pl.ds(b * PER * NX, PER * NX)] = total.astype(BF).reshape(PER * NX, SLOTS, SHARE)
        for p in range(b * PER, (b + 1) * PER):
            for dx in range(NX):
                src = eo.at[p * NX + (x + dx) % NX]
                dst = ret.at[p * NX + x]
                if (ORDER[p], dx) == (0, 0):
                    pltpu.make_async_copy(src, dst, r_recv.at[b]).start()
                else:
                    pltpu.make_async_remote_copy(
                        src_ref=src, dst_ref=dst, send_sem=r_send, recv_sem=r_recv.at[b],
                        device_id=at(ORDER[p], dx), device_id_type=MESH).start()

    stages = (gather, share, feed, scatter, give_back)
    for step in range(NB + len(stages) - 1):
        for lag in reversed(range(len(stages))):
            if 0 <= step - lag < NB:
                stages[lag](step - lag)

    mixed = jnp.zeros((256, SHARE), F32)
    for b in range(NB):
        wait_for(ret.at[pl.ds(b * PER * NX, PER * NX)], r_recv.at[b])
        block = ret[pl.ds(b * PER * NX, PER * NX)].reshape(B, SHARE)
        mixed = mixed + jnp.dot(qhi[:, b * B:(b + 1) * B], block, preferred_element_type=F32)
        mixed = mixed + jnp.dot(qlo[:, b * B:(b + 1) * B], block, preferred_element_type=F32)
    out[...] = mixed.astype(BF)

    wait_for(filled.at[pl.ds(0, NZ * NX - 1)], d_send)
    wait_for(g.at[0, pl.ds(0, 3)], a_send)
    wait_for(g.at[0], s_send)
    wait_for(sibp, p_send)
    wait_for(cs, y_send)
    wait_for(eo.at[pl.ds(0, NZ * NX - 1)], r_send)


def shards(tokens, routes, gate_weights, pad_mask, expand_weight, shrink_weight):
    vmem = pl.BlockSpec(memory_space=pltpu.VMEM)
    hbm = pl.BlockSpec(memory_space=pltpu.HBM)
    dma = pltpu.SemaphoreType.DMA
    return pl.pallas_call(
        kernel,
        out_shape=jax.ShapeDtypeStruct((256, SHARE), BF),
        in_specs=[hbm] * 6,
        out_specs=vmem,
        scratch_shapes=[
            pltpu.VMEM((256, SHARE), BF),
            pltpu.VMEM((2, 256), jnp.int32),
            pltpu.VMEM((2, 256), F32),
            pltpu.VMEM((1, 256), jnp.int32),
            pltpu.VMEM((2048, 512), BF),
            pltpu.VMEM((512, 2048), BF),
            pltpu.VMEM((NZ * NX, SLOTS, SHARE), BF),
            pltpu.VMEM((2, NY, ROWS, SHARE), BF),
            pltpu.VMEM((NB, 2, NY, B, SHARE), BF),
            pltpu.VMEM((NB, NY, B, SHARE), BF),
            pltpu.VMEM((NB, 3, B, SHARE), BF),
            pltpu.VMEM((NB, 3, B, SHARE), BF),
            pltpu.VMEM((NZ * NX, SLOTS, SHARE), BF),
            pltpu.VMEM((NZ * NX, SLOTS, SHARE), BF),
            pltpu.VMEM((256, ROWS), BF),
            pltpu.VMEM((256, ROWS), BF),
            dma((6,)),
            dma,
            dma((NB,)),
            dma,
            dma((NB, 3)),
            dma,
            dma((NB,)),
            dma,
            dma((NB,)),
            dma,
            dma((NB, 3)),
            dma,
            dma((NB,)),
        ],
        compiler_params=pltpu.CompilerParams(
            collective_id=0, has_side_effects=True, vmem_limit_bytes=63 * 2**20),
        cost_estimate=pl.CostEstimate(flops=4 * ROWS * 2048 * 512, bytes_accessed=5 * 2**20, transcendentals=0),
        name="moe",
    )(tokens, routes.T, gate_weights.T, pad_mask.reshape(1, 256), expand_weight, shrink_weight)


def solution(mesh):
    in_specs = (
        P("fsdp", "sec"),
        P("fsdp", None),
        P("fsdp", None),
        P("fsdp"),
        P("fsdp", None, "sec"),
        P("fsdp", "sec", None),
    )
    out_specs = P("fsdp", "sec")
    return jax.shard_map(shards, mesh=mesh, in_specs=in_specs, out_specs=out_specs, check_vma=False)
```

```python
import jax
import jax.numpy as jnp
from jax import lax
from jax.experimental import pallas as pl
from jax.experimental.pallas import tpu as pltpu
from jax.sharding import PartitionSpec as P

MESH = pl.DeviceIdType.MESH
NZ, NX, NY = 16, 4, 4
SLOTS = 16
SHARE = 256
ROWS = NZ * NX * SLOTS
BLOCKS = ((0, 14, 15), (1,), (4,), (5, 11), (8,), (10,), (12,), (7,), (13, 3), (9,), (2,), (6,))
STEPS = (
    (0, 1), (0, 0), (0, 2), (1, 0), (1, 1), (2, 1), (0, 3), (3, 1), (1, 2), (2, 2), (0, 4), (0, 5), (0, 6),
    (3, 2), (1, 3), (2, 3), (2, 0), (0, 8), (5, 1), (0, 7), (1, 4), (2, 4), (3, 3), (0, 10), (1, 5), (2, 5),
    (5, 2), (1, 6), (0, 9), (3, 0), (3, 4), (1, 8), (0, 11), (1, 7), (2, 7), (5, 3), (3, 5), (1, 10), (3, 7),
    (2, 6), (4, 0), (1, 9), (2, 9), (5, 4), (2, 8), (3, 6), (3, 9), (1, 11), (2, 11), (5, 5), (2, 10), (3, 8),
    (5, 7), (3, 11), (5, 0), (4, 6), (3, 10), (5, 9), (4, 8), (5, 11), (5, 6), (4, 10), (5, 8), (5, 10),
)
ORDER = sum(BLOCKS, ())
STEPS_FIRST = next(b for stage, b in STEPS if stage == 2)
NB = len(BLOCKS)
FIRST = tuple(sum(len(r) for r in BLOCKS[:b]) for b in range(NB + 1))
BLOCK_AT = tuple(b for b in range(NB) for _ in BLOCKS[b])
NEAR = 4
DIRECT = (0, 1, 1, 1, 1, 1, 0, 1, 0, 1, 0, 1)
EARLY = next(p for p in range(NZ) if min(ORDER[p], NZ - ORDER[p]) > NEAR)
BF = jnp.bfloat16
F32 = jnp.float32


def wait_for(ref, sem):
    pltpu.make_async_copy(ref, ref, sem).wait()


def kernel(tok_hbm, routes_hbm, gates_hbm, mask_hbm, w1_hbm, w2_hbm, out, tok, routes, gates, mask, w1, w2,
           filled, g, hown, hout, hsib, osum, cs, yrecv, hrecv, eo, ret, qhi, qlo, w_sem, w_send, w_recv, d_send,
           d_recv, a_send, a_recv, h_recv, p_send, p_recv, y_send, y_recv, e_recv, r_send, r_recv, far_in):
    sec = lax.axis_index("sec")
    fs = lax.axis_index("fsdp")
    y, c = sec // 2, sec % 2
    z, x = fs // NX, fs % NX
    sib = (y * 2 + (1 - c), fs)

    def at(dz, dx):
        return (sec, (z + dz) % NZ * NX + (x + dx) % NX)

    def at_y(dy):
        return ((y + dy) % NY * 2 + c, fs)

    barrier = pltpu.get_barrier_semaphore()
    partners = [at(dz, dx) for d in range(NEAR, -1, -1) for dz in sorted({d, (NZ - d) % NZ}) for dx in range(NX) if (dz, dx) != (0, 0)]
    partners += [at_y(1), at_y(2), at_y(3), sib]
    for partner in partners:
        pl.semaphore_signal(barrier, inc=1, device_id=partner, device_id_type=MESH)

    def strips(parity, to):
        for k in range(NY):
            start = pl.multiple_of((k * 2 + parity) * SHARE, SHARE)
            here = pl.ds(k * SHARE, SHARE)
            to(w1_hbm.at[0, pl.ds(start, SHARE)], w1.at[c, here], 0)
            to(w2_hbm.at[0, :, pl.ds(start, SHARE)], w2.at[c, :, here], 1)

    strips(c, lambda src, dst, k: pltpu.make_async_copy(src, dst, w_sem.at[k]).start())
    loads = [pltpu.make_async_copy(src, dst, w_sem.at[2 + i]) for i, (src, dst) in enumerate(
        ((routes_hbm, routes), (tok_hbm, tok), (gates_hbm, gates), (mask_hbm, mask)))]
    for load in loads:
        load.start()
    for load in loads[:2]:
        load.wait()

    ids = routes[...]
    expert = lax.broadcasted_iota(jnp.int32, (NZ * NX, 256), 0)
    named = [(expert == ids[k:k + 1, :]).astype(F32) for k in range(2)]
    row = lax.broadcasted_iota(jnp.int32, (256, 256), 0)
    col = lax.broadcasted_iota(jnp.int32, (256, 256), 1)
    earlier = ((row < col) & (row // 128 == col // 128)).astype(BF)
    before = jnp.dot((named[0] + named[1]).astype(BF), earlier, preferred_element_type=F32)
    away = (z - (ids >> 2)) & (NZ - 1)
    place = jnp.zeros_like(ids)
    for p, r in enumerate(ORDER):
        place = jnp.where(away == r, p, place)
    half = lax.broadcasted_iota(jnp.int32, (1, 256), 1) // 128
    target = []
    for k in range(2):
        rank = jnp.sum(named[k] * before, axis=0, keepdims=True).astype(jnp.int32)
        target.append(place[k:k + 1, :] * (NX * SLOTS) + (ids[k:k + 1, :] & (NX - 1)) * SLOTS + half * 8 + rank)
    slot = lax.broadcasted_iota(jnp.int32, (ROWS, 256), 0)
    pick = ((slot == target[0]) | (slot == target[1])).astype(BF)
    filled[...] = jnp.dot(pick, tok[...], preferred_element_type=F32).astype(BF).reshape(NZ * NX, SLOTS, SHARE)

    pl.semaphore_wait(barrier, len(partners))
    pl.semaphore_signal(far_in.at[0], inc=1, device_id=at(NEAR, 0), device_id_type=MESH)
    pl.semaphore_signal(far_in.at[1], inc=1, device_id=at(NZ - NEAR, 0), device_id_type=MESH)

    def rows(b):
        return pl.ds(FIRST[b] * NX * SLOTS, len(BLOCKS[b]) * NX * SLOTS)

    def chunks(b):
        return pl.ds(FIRST[b] * NX, len(BLOCKS[b]) * NX)

    def dispatch(places):
        for p in places:
            r = ORDER[p]
            for dx in range(NX):
                src = filled.at[p * NX + (x + dx) % NX]
                dst = g.at[y, pl.ds(pl.multiple_of((p * NX + x) * SLOTS, SLOTS), SLOTS)]
                if (r, dx) == (0, 0):
                    pltpu.make_async_copy(src, dst, d_recv.at[BLOCK_AT[p]]).start()
                else:
                    pltpu.make_async_remote_copy(
                        src_ref=src, dst_ref=dst, send_sem=d_send, recv_sem=d_recv.at[BLOCK_AT[p]],
                        device_id=at(NZ - r, dx), device_id_type=MESH).start()

    dispatch(range(EARLY))
    strips(1 - c, lambda src, dst, k: pltpu.make_async_remote_copy(
        src_ref=src, dst_ref=dst, send_sem=w_send.at[k], recv_sem=w_recv.at[k], device_id=sib,
        device_id_type=MESH).start())

    for load in loads[2:]:
        load.wait()
    scale = gates[...] * mask[...].astype(F32)
    lanes = jnp.concatenate([target[0].astype(F32), target[1].astype(F32), scale, jnp.zeros((124, 256), F32)], axis=0)
    sides = lanes.T
    column = lax.broadcasted_iota(jnp.int32, (256, ROWS), 1)
    q = jnp.where(column == sides[:, 0:1].astype(jnp.int32), sides[:, 2:3], 0.0)
    q = q + jnp.where(column == sides[:, 1:2].astype(jnp.int32), sides[:, 3:4], 0.0)
    high = q.astype(BF)
    qhi[...] = high
    qlo[...] = (q - high.astype(F32)).astype(BF)

    pl.semaphore_wait(far_in.at[0], 1)
    pl.semaphore_wait(far_in.at[1], 1)
    dispatch(range(EARLY, NZ))

    def send(src, dst, send_sem, recv_sem, device):
        pltpu.make_async_remote_copy(
            src_ref=src, dst_ref=dst, send_sem=send_sem, recv_sem=recv_sem, device_id=device,
            device_id_type=MESH).start()

    def first(b):
        return pl.ds(FIRST[b] * NX * SLOTS, len(BLOCKS[b]) * NX * SLOTS // 2)

    def second(b):
        half = len(BLOCKS[b]) * NX * SLOTS // 2
        return pl.ds(FIRST[b] * NX * SLOTS + half, half)

    up, down, across = (y + 1) % NY, (y + NY - 1) % NY, (y + 2) % NY

    def gather(b):
        own = g.at[y, rows(b)]
        wait_for(own, d_recv.at[b])
        send(own, own, a_send, a_recv.at[b, 0], at_y(1))
        send(own, own, a_send, a_recv.at[b, 1], at_y(3))
        if DIRECT[b]:
            send(own, own, a_send, h_recv.at[b, 0], at_y(2))

    def relay(b):
        for k, (origin, half, dy) in enumerate(((down, first(b), 1), (up, second(b), 3))):
            wait_for(g.at[origin, rows(b)], a_recv.at[b, k])
            if not DIRECT[b]:
                part_of = g.at[origin, half]
                send(part_of, part_of, a_send, h_recv.at[b, k], at_y(dy))

    def expand(b):
        if DIRECT[b]:
            wait_for(g.at[across, rows(b)], h_recv.at[b, 0])
        else:
            wait_for(g.at[across, first(b)], h_recv.at[b, 0])
            wait_for(g.at[across, second(b)], h_recv.at[b, 1])
        if b == STEPS_FIRST:
            wait_for(w1.at[c], w_sem.at[0])
            wait_for(w2.at[c], w_sem.at[1])
            wait_for(w1.at[1 - c], w_recv.at[0])
            wait_for(w2.at[1 - c], w_recv.at[1])
        xs = jnp.concatenate([g[k, rows(b), :] for k in range(NY)], axis=1)
        for j in range(2):
            units = jnp.dot(xs, w1[j], preferred_element_type=F32)
            hown[j, rows(b), :] = units
            hout[j, rows(b), :] = units.astype(BF)
        send(hout.at[:, rows(b)], hsib.at[:, rows(b)], p_send, p_recv.at[b], sib)

    def shrink(b):
        wait_for(hsib.at[:, rows(b)], p_recv.at[b])
        total = None
        for j in range(2):
            hidden = jnp.maximum(hown[j, rows(b), :] + hsib[j, rows(b), :].astype(F32), 0.0).astype(BF)
            term = jnp.dot(hidden, w2[j], preferred_element_type=F32)
            total = term if total is None else total + term
        for k in range(NY):
            osum[k, rows(b), :] = total[:, k * SHARE:(k + 1) * SHARE]
        cs[1, rows(b), :] = osum[across, rows(b), :].astype(BF)
        if DIRECT[b]:
            send(cs.at[1, rows(b)], hrecv.at[rows(b)], y_send, e_recv.at[b, 0], at_y(2))
            for k, (strip, dy) in enumerate(((up, 1), (down, 3))):
                cs[2 * k, rows(b), :] = osum[strip, rows(b), :].astype(BF)
                send(cs.at[2 * k, rows(b)], yrecv.at[k, rows(b)], y_send, y_recv.at[b, k], at_y(dy))
        else:
            send(cs.at[1, first(b)], hrecv.at[first(b)], y_send, e_recv.at[b, 0], at_y(1))
            send(cs.at[1, second(b)], hrecv.at[second(b)], y_send, e_recv.at[b, 1], at_y(3))

    def pass_on(b):
        if DIRECT[b]:
            return
        for k, (strip, here, other, dy) in enumerate(((up, first(b), second(b), 1), (down, second(b), first(b), 3))):
            cs[2 * k, other, :] = osum[strip, other, :].astype(BF)
            wait_for(hrecv.at[here], e_recv.at[b, k])
            cs[2 * k, here, :] = (osum[strip, here, :] + hrecv[here, :].astype(F32)).astype(BF)
            send(cs.at[2 * k, rows(b)], yrecv.at[k, rows(b)], y_send, y_recv.at[b, k], at_y(dy))

    def give_back(b):
        total = osum[y, rows(b), :]
        if DIRECT[b]:
            wait_for(hrecv.at[rows(b)], e_recv.at[b, 0])
            total = total + hrecv[rows(b), :].astype(F32)
        for k in range(2):
            wait_for(yrecv.at[k, rows(b)], y_recv.at[b, k])
            total = total + yrecv[k, rows(b), :].astype(F32)
        eo[chunks(b)] = total.astype(BF).reshape(len(BLOCKS[b]) * NX, SLOTS, SHARE)
        for p in range(FIRST[b], FIRST[b + 1]):
            for dx in range(NX):
                src = eo.at[p * NX + (x + dx) % NX]
                dst = ret.at[p * NX + x]
                if (ORDER[p], dx) == (0, 0):
                    pltpu.make_async_copy(src, dst, r_recv.at[b]).start()
                else:
                    pltpu.make_async_remote_copy(
                        src_ref=src, dst_ref=dst, send_sem=r_send, recv_sem=r_recv.at[b],
                        device_id=at(ORDER[p], dx), device_id_type=MESH).start()

    stages = (gather, relay, expand, shrink, pass_on, give_back)
    for stage, b in STEPS:
        stages[stage](b)

    mixed = jnp.zeros((256, SHARE), F32)
    for b in range(NB):
        wait_for(ret.at[chunks(b)], r_recv.at[b])
        block = ret[chunks(b)].reshape(len(BLOCKS[b]) * NX * SLOTS, SHARE)
        mixed = mixed + jnp.dot(qhi[:, rows(b)], block, preferred_element_type=F32)
        mixed = mixed + jnp.dot(qlo[:, rows(b)], block, preferred_element_type=F32)
    out[...] = mixed.astype(BF)

    wait_for(filled.at[pl.ds(0, NZ * NX - 1)], d_send)
    wait_for(g.at[pl.ds(0, 3)], a_send)
    wait_for(hout, p_send)
    wait_for(w1.at[0], w_send.at[0])
    wait_for(w2.at[0], w_send.at[1])
    wait_for(cs, y_send)
    wait_for(eo.at[pl.ds(0, NZ * NX - 1)], r_send)


def shards(tokens, routes, gate_weights, pad_mask, expand_weight, shrink_weight):
    vmem = pl.BlockSpec(memory_space=pltpu.VMEM)
    hbm = pl.BlockSpec(memory_space=pltpu.HBM)
    dma = pltpu.SemaphoreType.DMA
    return pl.pallas_call(
        kernel,
        out_shape=jax.ShapeDtypeStruct((256, SHARE), BF),
        in_specs=[hbm] * 6,
        out_specs=vmem,
        scratch_shapes=[
            pltpu.VMEM((256, SHARE), BF),
            pltpu.VMEM((2, 256), jnp.int32),
            pltpu.VMEM((2, 256), F32),
            pltpu.VMEM((1, 256), jnp.int32),
            pltpu.VMEM((2, NY * SHARE, 512), BF),
            pltpu.VMEM((2, 512, NY * SHARE), BF),
            pltpu.VMEM((NZ * NX, SLOTS, SHARE), BF),
            pltpu.VMEM((NY, ROWS, SHARE), BF),
            pltpu.VMEM((2, ROWS, 512), F32),
            pltpu.VMEM((2, ROWS, 512), BF),
            pltpu.VMEM((2, ROWS, 512), BF),
            pltpu.VMEM((NY, ROWS, SHARE), F32),
            pltpu.VMEM((3, ROWS, SHARE), BF),
            pltpu.VMEM((2, ROWS, SHARE), BF),
            pltpu.VMEM((ROWS, SHARE), BF),
            pltpu.VMEM((NZ * NX, SLOTS, SHARE), BF),
            pltpu.VMEM((NZ * NX, SLOTS, SHARE), BF),
            pltpu.VMEM((256, ROWS), BF),
            pltpu.VMEM((256, ROWS), BF),
            dma((6,)),
            dma((2,)),
            dma((2,)),
            dma,
            dma((NB,)),
            dma,
            dma((NB, 2)),
            dma((NB, 2)),
            dma,
            dma((NB,)),
            dma,
            dma((NB, 2)),
            dma((NB, 2)),
            dma,
            dma((NB,)),
            pltpu.SemaphoreType.REGULAR((2,)),
        ],
        compiler_params=pltpu.CompilerParams(
            collective_id=0, has_side_effects=True, vmem_limit_bytes=63 * 2**20),
        cost_estimate=pl.CostEstimate(flops=4 * ROWS * 2048 * 512, bytes_accessed=5 * 2**20, transcendentals=0),
        name="moe",
    )(tokens, routes.T, gate_weights.T, pad_mask.reshape(1, 256), expand_weight, shrink_weight)


def solution(mesh):
    in_specs = (
        P("fsdp", "sec"),
        P("fsdp", None),
        P("fsdp", None),
        P("fsdp"),
        P("fsdp", None, "sec"),
        P("fsdp", "sec", None),
    )
    out_specs = P("fsdp", "sec")
    return jax.shard_map(shards, mesh=mesh, in_specs=in_specs, out_specs=out_specs, check_vma=False)
```

```python
import jax
import jax.numpy as jnp
from jax import lax
from jax.experimental import pallas as pl
from jax.experimental.pallas import tpu as pltpu
from jax.sharding import PartitionSpec as P

MESH = pl.DeviceIdType.MESH
NZ, NX, NY = 16, 4, 4
SLOTS = 16
SHARE = 256
ROWS = NZ * NX * SLOTS
BLOCKS = ((2,), (4,), (12,), (8,), (14,), (0, 1), (7, 9), (6, 11), (13, 3, 15), (5,), (10,))
STEPS = (
    (0, 0), (0, 2), (0, 1), (0, 5), (1, 0), (2, 0), (0, 4), (1, 2), (2, 2), (0, 3), (1, 1), (2, 1), (1, 5),
    (3, 0), (1, 4), (3, 2), (3, 1), (0, 6), (1, 3), (2, 3), (2, 5), (2, 4), (0, 7), (3, 3), (5, 0), (5, 2),
    (5, 1), (0, 8), (3, 4), (0, 9), (1, 6), (2, 6), (1, 7), (0, 10), (3, 5), (1, 8), (3, 6), (4, 4), (5, 3),
    (1, 9), (2, 9), (2, 7), (4, 5), (1, 10), (2, 10), (2, 8), (3, 9), (3, 7), (5, 6), (3, 10), (5, 4), (3, 8),
    (5, 5), (5, 9), (4, 7), (5, 10), (4, 8), (5, 7), (5, 8),
)
ORDER = sum(BLOCKS, ())
STEPS_FIRST = next(b for stage, b in STEPS if stage == 2)
NB = len(BLOCKS)
FIRST = tuple(sum(len(r) for r in BLOCKS[:b]) for b in range(NB + 1))
BLOCK_AT = tuple(b for b in range(NB) for _ in BLOCKS[b])
NEAR = 4
DIRECT = (1, 1, 1, 1, 0, 0, 1, 0, 0, 1, 1)
EARLY = next(p for p in range(NZ) if min(ORDER[p], NZ - ORDER[p]) > NEAR)
BF = jnp.bfloat16
F32 = jnp.float32


def wait_for(ref, sem):
    pltpu.make_async_copy(ref, ref, sem).wait()


def kernel(tok_hbm, routes_hbm, gates_hbm, mask_hbm, w1_hbm, w2_hbm, out, tok, routes, gates, mask, w1, w2,
           filled, g, hown, hout, hsib, osum, cs, yrecv, hrecv, eo, ret, qhi, qlo, w_sem, w_send, w_recv, d_send,
           d_recv, a_send, a_recv, h_recv, p_send, p_recv, y_send, y_recv, e_recv, r_send, r_recv, far_in):
    sec = lax.axis_index("sec")
    fs = lax.axis_index("fsdp")
    y, c = sec // 2, sec % 2
    z, x = fs // NX, fs % NX
    sib = (y * 2 + (1 - c), fs)

    def at(dz, dx):
        return (sec, (z + dz) % NZ * NX + (x + dx) % NX)

    def at_y(dy):
        return ((y + dy) % NY * 2 + c, fs)

    loads = [pltpu.make_async_copy(src, dst, w_sem.at[2 + i]) for i, (src, dst) in enumerate(
        ((routes_hbm, routes), (tok_hbm, tok), (gates_hbm, gates), (mask_hbm, mask)))]
    for load in loads:
        load.start()

    barrier = pltpu.get_barrier_semaphore()
    partners = [at(dz, dx) for d in range(NEAR, -1, -1) for dz in sorted({d, (NZ - d) % NZ}) for dx in range(NX) if (dz, dx) != (0, 0)]
    partners += [at_y(1), at_y(2), at_y(3), sib]
    for partner in partners:
        pl.semaphore_signal(barrier, inc=1, device_id=partner, device_id_type=MESH)

    def strips(parity, to):
        for k in range(NY):
            start = pl.multiple_of((k * 2 + parity) * SHARE, SHARE)
            here = pl.ds(k * SHARE, SHARE)
            to(w1_hbm.at[0, pl.ds(start, SHARE)], w1.at[c, here], 0)
            to(w2_hbm.at[0, :, pl.ds(start, SHARE)], w2.at[c, :, here], 1)

    row = lax.broadcasted_iota(jnp.int32, (256, 256), 0)
    col = lax.broadcasted_iota(jnp.int32, (256, 256), 1)
    earlier = ((row < col) & (row // 128 == col // 128)).astype(BF)
    for load in loads[:2]:
        load.wait()

    ids = routes[...]
    expert = lax.broadcasted_iota(jnp.int32, (NZ * NX, 256), 0)
    named = [(expert == ids[k:k + 1, :]).astype(F32) for k in range(2)]
    before = jnp.dot((named[0] + named[1]).astype(BF), earlier, preferred_element_type=F32)
    away = (z - (ids >> 2)) & (NZ - 1)
    place = jnp.zeros_like(ids)
    for p, r in enumerate(ORDER):
        place = jnp.where(away == r, p, place)
    half = lax.broadcasted_iota(jnp.int32, (1, 256), 1) // 128
    target = []
    for k in range(2):
        rank = jnp.sum(named[k] * before, axis=0, keepdims=True).astype(jnp.int32)
        target.append(place[k:k + 1, :] * (NX * SLOTS) + (ids[k:k + 1, :] & (NX - 1)) * SLOTS + half * 8 + rank)
    def fill(start, stop):
        slot = lax.broadcasted_iota(jnp.int32, ((stop - start) * NX * SLOTS, 256), 0) + start * NX * SLOTS
        pick = ((slot == target[0]) | (slot == target[1])).astype(BF)
        held = jnp.dot(pick, tok[...], preferred_element_type=F32).astype(BF)
        filled[pl.ds(start * NX, (stop - start) * NX)] = held.reshape((stop - start) * NX, SLOTS, SHARE)

    fill(0, EARLY)
    pl.semaphore_wait(barrier, len(partners))
    pl.semaphore_signal(far_in.at[0], inc=1, device_id=at(NEAR, 0), device_id_type=MESH)
    pl.semaphore_signal(far_in.at[1], inc=1, device_id=at(NZ - NEAR, 0), device_id_type=MESH)

    def rows(b):
        return pl.ds(FIRST[b] * NX * SLOTS, len(BLOCKS[b]) * NX * SLOTS)

    def chunks(b):
        return pl.ds(FIRST[b] * NX, len(BLOCKS[b]) * NX)

    def dispatch(places):
        for p in places:
            r = ORDER[p]
            for dx in range(NX):
                src = filled.at[p * NX + (x + dx) % NX]
                dst = g.at[y, pl.ds(pl.multiple_of((p * NX + x) * SLOTS, SLOTS), SLOTS)]
                if (r, dx) == (0, 0):
                    pltpu.make_async_copy(src, dst, d_recv.at[BLOCK_AT[p]]).start()
                else:
                    pltpu.make_async_remote_copy(
                        src_ref=src, dst_ref=dst, send_sem=d_send, recv_sem=d_recv.at[BLOCK_AT[p]],
                        device_id=at(NZ - r, dx), device_id_type=MESH).start()

    dispatch(range(EARLY))
    strips(c, lambda src, dst, k: pltpu.make_async_copy(src, dst, w_sem.at[k]).start())
    strips(1 - c, lambda src, dst, k: pltpu.make_async_remote_copy(
        src_ref=src, dst_ref=dst, send_sem=w_send.at[k], recv_sem=w_recv.at[k], device_id=sib,
        device_id_type=MESH).start())

    fill(EARLY, NZ)

    for load in loads[2:]:
        load.wait()
    scale = gates[...] * mask[...].astype(F32)
    lanes = jnp.concatenate([target[0].astype(F32), target[1].astype(F32), scale, jnp.zeros((124, 256), F32)], axis=0)
    sides = lanes.T
    column = lax.broadcasted_iota(jnp.int32, (256, ROWS), 1)
    q = jnp.where(column == sides[:, 0:1].astype(jnp.int32), sides[:, 2:3], 0.0)
    q = q + jnp.where(column == sides[:, 1:2].astype(jnp.int32), sides[:, 3:4], 0.0)
    high = q.astype(BF)
    qhi[...] = high
    qlo[...] = (q - high.astype(F32)).astype(BF)

    pl.semaphore_wait(far_in.at[0], 1)
    pl.semaphore_wait(far_in.at[1], 1)
    dispatch(range(EARLY, NZ))

    def send(src, dst, send_sem, recv_sem, device):
        pltpu.make_async_remote_copy(
            src_ref=src, dst_ref=dst, send_sem=send_sem, recv_sem=recv_sem, device_id=device,
            device_id_type=MESH).start()

    def first(b):
        return pl.ds(FIRST[b] * NX * SLOTS, len(BLOCKS[b]) * NX * SLOTS // 2)

    def second(b):
        half = len(BLOCKS[b]) * NX * SLOTS // 2
        return pl.ds(FIRST[b] * NX * SLOTS + half, half)

    up, down, across = (y + 1) % NY, (y + NY - 1) % NY, (y + 2) % NY

    def gather(b):
        own = g.at[y, rows(b)]
        wait_for(own, d_recv.at[b])
        send(own, own, a_send, a_recv.at[b, 0], at_y(1))
        send(own, own, a_send, a_recv.at[b, 1], at_y(3))
        if DIRECT[b]:
            send(own, own, a_send, h_recv.at[b, 0], at_y(2))

    def relay(b):
        for k, (origin, half, dy) in enumerate(((down, first(b), 1), (up, second(b), 3))):
            wait_for(g.at[origin, rows(b)], a_recv.at[b, k])
            if not DIRECT[b]:
                part_of = g.at[origin, half]
                send(part_of, part_of, a_send, h_recv.at[b, k], at_y(dy))

    def expand(b):
        if DIRECT[b]:
            wait_for(g.at[across, rows(b)], h_recv.at[b, 0])
        else:
            wait_for(g.at[across, first(b)], h_recv.at[b, 0])
            wait_for(g.at[across, second(b)], h_recv.at[b, 1])
        if b == STEPS_FIRST:
            wait_for(w1.at[c], w_sem.at[0])
            wait_for(w2.at[c], w_sem.at[1])
            wait_for(w1.at[1 - c], w_recv.at[0])
            wait_for(w2.at[1 - c], w_recv.at[1])
        xs = jnp.concatenate([g[k, rows(b), :] for k in range(NY)], axis=1)
        for j in range(2):
            units = jnp.dot(xs, w1[j], preferred_element_type=F32)
            hown[j, rows(b), :] = units
            hout[j, rows(b), :] = units.astype(BF)
        send(hout.at[:, rows(b)], hsib.at[:, rows(b)], p_send, p_recv.at[b], sib)

    def shrink(b):
        wait_for(hsib.at[:, rows(b)], p_recv.at[b])
        total = None
        for j in range(2):
            hidden = jnp.maximum(hown[j, rows(b), :] + hsib[j, rows(b), :].astype(F32), 0.0).astype(BF)
            term = jnp.dot(hidden, w2[j], preferred_element_type=F32)
            total = term if total is None else total + term
        for k in range(NY):
            osum[k, rows(b), :] = total[:, k * SHARE:(k + 1) * SHARE]
        cs[1, rows(b), :] = osum[across, rows(b), :].astype(BF)
        if DIRECT[b]:
            send(cs.at[1, rows(b)], hrecv.at[rows(b)], y_send, e_recv.at[b, 0], at_y(2))
            for k, (strip, dy) in enumerate(((up, 1), (down, 3))):
                cs[2 * k, rows(b), :] = osum[strip, rows(b), :].astype(BF)
                send(cs.at[2 * k, rows(b)], yrecv.at[k, rows(b)], y_send, y_recv.at[b, k], at_y(dy))
        else:
            send(cs.at[1, first(b)], hrecv.at[first(b)], y_send, e_recv.at[b, 0], at_y(1))
            send(cs.at[1, second(b)], hrecv.at[second(b)], y_send, e_recv.at[b, 1], at_y(3))

    def pass_on(b):
        if DIRECT[b]:
            return
        for k, (strip, here, other, dy) in enumerate(((up, first(b), second(b), 1), (down, second(b), first(b), 3))):
            cs[2 * k, other, :] = osum[strip, other, :].astype(BF)
            wait_for(hrecv.at[here], e_recv.at[b, k])
            cs[2 * k, here, :] = (osum[strip, here, :] + hrecv[here, :].astype(F32)).astype(BF)
            send(cs.at[2 * k, rows(b)], yrecv.at[k, rows(b)], y_send, y_recv.at[b, k], at_y(dy))

    def give_back(b):
        total = osum[y, rows(b), :]
        if DIRECT[b]:
            wait_for(hrecv.at[rows(b)], e_recv.at[b, 0])
            total = total + hrecv[rows(b), :].astype(F32)
        for k in range(2):
            wait_for(yrecv.at[k, rows(b)], y_recv.at[b, k])
            total = total + yrecv[k, rows(b), :].astype(F32)
        eo[chunks(b)] = total.astype(BF).reshape(len(BLOCKS[b]) * NX, SLOTS, SHARE)
        for p in range(FIRST[b], FIRST[b + 1]):
            for dx in range(NX):
                src = eo.at[p * NX + (x + dx) % NX]
                dst = ret.at[p * NX + x]
                if (ORDER[p], dx) == (0, 0):
                    pltpu.make_async_copy(src, dst, r_recv.at[b]).start()
                else:
                    pltpu.make_async_remote_copy(
                        src_ref=src, dst_ref=dst, send_sem=r_send, recv_sem=r_recv.at[b],
                        device_id=at(ORDER[p], dx), device_id_type=MESH).start()

    stages = (gather, relay, expand, shrink, pass_on, give_back)
    for stage, b in STEPS:
        stages[stage](b)

    mixed = jnp.zeros((256, SHARE), F32)
    for b in range(NB):
        wait_for(ret.at[chunks(b)], r_recv.at[b])
        block = ret[chunks(b)].reshape(len(BLOCKS[b]) * NX * SLOTS, SHARE)
        mixed = mixed + jnp.dot(qhi[:, rows(b)], block, preferred_element_type=F32)
        mixed = mixed + jnp.dot(qlo[:, rows(b)], block, preferred_element_type=F32)
    out[...] = mixed.astype(BF)

    wait_for(filled.at[pl.ds(0, NZ * NX - 1)], d_send)
    wait_for(g.at[pl.ds(0, 3)], a_send)
    wait_for(hout, p_send)
    wait_for(w1.at[0], w_send.at[0])
    wait_for(w2.at[0], w_send.at[1])
    wait_for(cs, y_send)
    wait_for(eo.at[pl.ds(0, NZ * NX - 1)], r_send)


def shards(tokens, routes, gate_weights, pad_mask, expand_weight, shrink_weight):
    vmem = pl.BlockSpec(memory_space=pltpu.VMEM)
    hbm = pl.BlockSpec(memory_space=pltpu.HBM)
    dma = pltpu.SemaphoreType.DMA
    return pl.pallas_call(
        kernel,
        out_shape=jax.ShapeDtypeStruct((256, SHARE), BF),
        in_specs=[hbm] * 6,
        out_specs=vmem,
        scratch_shapes=[
            pltpu.VMEM((256, SHARE), BF),
            pltpu.VMEM((2, 256), jnp.int32),
            pltpu.VMEM((2, 256), F32),
            pltpu.VMEM((1, 256), jnp.int32),
            pltpu.VMEM((2, NY * SHARE, 512), BF),
            pltpu.VMEM((2, 512, NY * SHARE), BF),
            pltpu.VMEM((NZ * NX, SLOTS, SHARE), BF),
            pltpu.VMEM((NY, ROWS, SHARE), BF),
            pltpu.VMEM((2, ROWS, 512), F32),
            pltpu.VMEM((2, ROWS, 512), BF),
            pltpu.VMEM((2, ROWS, 512), BF),
            pltpu.VMEM((NY, ROWS, SHARE), F32),
            pltpu.VMEM((3, ROWS, SHARE), BF),
            pltpu.VMEM((2, ROWS, SHARE), BF),
            pltpu.VMEM((ROWS, SHARE), BF),
            pltpu.VMEM((NZ * NX, SLOTS, SHARE), BF),
            pltpu.VMEM((NZ * NX, SLOTS, SHARE), BF),
            pltpu.VMEM((256, ROWS), BF),
            pltpu.VMEM((256, ROWS), BF),
            dma((6,)),
            dma((2,)),
            dma((2,)),
            dma,
            dma((NB,)),
            dma,
            dma((NB, 2)),
            dma((NB, 2)),
            dma,
            dma((NB,)),
            dma,
            dma((NB, 2)),
            dma((NB, 2)),
            dma,
            dma((NB,)),
            pltpu.SemaphoreType.REGULAR((2,)),
        ],
        compiler_params=pltpu.CompilerParams(
            collective_id=0, has_side_effects=True, vmem_limit_bytes=63 * 2**20),
        cost_estimate=pl.CostEstimate(flops=4 * ROWS * 2048 * 512, bytes_accessed=5 * 2**20, transcendentals=0),
        name="moe",
    )(tokens, routes.T, gate_weights.T, pad_mask.reshape(1, 256), expand_weight, shrink_weight)


def solution(mesh):
    in_specs = (
        P("fsdp", "sec"),
        P("fsdp", None),
        P("fsdp", None),
        P("fsdp"),
        P("fsdp", None, "sec"),
        P("fsdp", "sec", None),
    )
    out_specs = P("fsdp", "sec")
    return jax.shard_map(shards, mesh=mesh, in_specs=in_specs, out_specs=out_specs, check_vma=False)
```
